128 devices in a mesh: row: 4 (over z_hi, core), col: 8 (over x, z_lo), depth: 4 (over y).
Axes of the slice: x: 4, y: 4, z: 4 (z_hi: 2, z_lo: 2; z = z_hi * 2 + z_lo), core: 2. Of those that a mesh axis runs over, the one named last changes fastest.
Arguments:
- activations: bfloat16 [3072, 8192], P(('row', 'depth'), 'col'), may hold values from -6 to 6
- grad_output: bfloat16 [3072, 28672], P('col', ('row', 'depth')), may hold values from -0.75 to 0.75
- weight: bfloat16 [28672, 8192], P(('row', 'depth'), 'col'), may hold values from -0.0625 to 0.0625
Outputs:
- grad_input: bfloat16 [3072, 8192], P(('row', 'depth'), 'col')
- grad_weight: bfloat16 [28672, 8192], P(('row', 'depth'), 'col')
The draws below stay inside these ranges and needn't reach their ends.
All inputs are finite; a program needn't handle non-finite values.
Results may differ from the reference program's by a relative error of at most 0.019.
Values may be sent and summed in bfloat16 or wider, within the bound.
No kernel may reach another device: no remote copies, remote signals or barrier semaphores. Data moves between devices by JAX's collectives and lax.ppermute only.
A program may use at most 128 MiB of HBM per device.

```python
import jax
import jax.numpy as jnp

D = 8192
FF = 28672
TOKENS = 3072
N_ROW = 4
N_DEPTH = 4


def spiked(result, own_key, source, target, blocks, factor):
    def block_of(axis_at):
        return (jnp.arange(result.shape[axis_at]) // (result.shape[axis_at] // blocks)).reshape((-1,) + (1,) * (result.ndim - 1 - axis_at))

    one_side = jax.random.permutation(own_key, blocks)[block_of(target)]
    other_side = (block_of(target) + blocks // 2) % blocks
    return jnp.where((block_of(source) == one_side) | (block_of(source) == other_side), factor * result, result)


def shard_levels(stream_key, shape, cuts, low, high):
    loudness, own = 1.0, jax.random.fold_in(stream_key, 6)
    for axis_at, shards_of in cuts:
        heights = jnp.exp(jax.random.uniform(jax.random.fold_in(own, axis_at), (shards_of,), jnp.float32, low / len(cuts), high / len(cuts)))
        loudness = loudness * jnp.repeat(heights, shape[axis_at] // shards_of).reshape([-1 if axis == axis_at else 1 for axis in range(len(shape))])
    return loudness


def scatter_about(own_key, dims, scale, reach, shards=(), held_as=jnp.bfloat16):
    gain = shard_levels(own_key, dims, shards, -0.22, 0.18) if shards else 1.0
    entries = jax.random.normal(own_key, dims, jnp.float32) * scale * gain
    return jnp.minimum(jnp.maximum(entries, -reach), reach).astype(held_as)


def noise_with(key, extent, deviation, limit, split, heavy, dtype=jnp.bfloat16):
    drawn = deviation * jax.random.normal(key, extent, jnp.float32)
    if split:
        drawn = drawn * shard_levels(key, extent, split, -0.22, 0.18)
    return jnp.clip(spiked(drawn, jax.random.fold_in(key, 3), *heavy), -limit, limit).astype(dtype)


def setup_inputs(seed: int = 0) -> dict:
    seeds = jax.random.split(jax.random.key(seed), 4)
    return {
        "activations": noise_with(seeds[0], (TOKENS, D), 1.0, 6.0, ((0, 16), (1, 8)), (0, 1, 16, 2.0)),
        "grad_output": noise_with(seeds[1], (TOKENS, FF), 0.125, 0.75, ((0, 8), (1, 16)), (1, 0, 16, 2.0)),
        "weight": scatter_about(seeds[2], (FF, D), D ** -0.5, 0.0625, ((0, 16), (1, 8))),
    }


def reference(activations, grad_output, weight):
    groups = N_ROW * N_DEPTH
    block = FF // groups
    total = jnp.zeros((TOKENS, D), jnp.float32)
    for index in range(groups):
        lower = index * block
        partial_block = jnp.dot(grad_output[:, lower:lower + block], weight[lower:lower + block, :], preferred_element_type=jnp.float32)
        total = total + partial_block.astype(jnp.bfloat16).astype(jnp.float32)
    grad_input = total.astype(jnp.bfloat16)
    product = jnp.dot(grad_output.T, activations, preferred_element_type=jnp.float32)
    grad_weight = product.astype(jnp.bfloat16)
    return grad_input, grad_weight
```

```python
import functools

import jax
import jax.numpy as jnp
from jax import lax
from jax.experimental import pallas as pl
from jax.experimental.pallas import tpu as pltpu
from jax.sharding import PartitionSpec as P

BLOCK = 192
PARTS = ((0, 96), (96, 96))
VMEM_LIMIT = 48 * 1024 * 1024

PIECES = (
    ((0, 0, 0), (0, 0, 1)),
    ((3, 0, 0), (3, 0, 1)),
    ((1, 0, 0), (1, 0, 1)),
    ((0, 1, 0), (0, 1, 1)),
    ((2, 0, 0), (3, 1, 0)),
    ((2, 0, 1), (1, 1, 0)),
    ((1, 1, 1), (3, 1, 1)),
    ((2, 1, 0),),
    ((2, 1, 1),),
)


def source_of(shift, flip):
    col = lax.axis_index("col")
    x = lax.rem(col // 2 + shift, 4)
    z = lax.rem(col + flip, 2)
    return x, z


def grad_input_kernel(n, *refs):
    count = len(PIECES)
    chunks, w_hbm = refs[:count], refs[count]
    keep, send = refs[count + 1], refs[count + 2]
    w, g, w_sem, g_sem = refs[count + 3:]
    row, y = lax.axis_index("row"), lax.axis_index("depth")
    w_copy = pltpu.make_async_copy(w_hbm, w, w_sem)
    w_copy.start()
    copies, at, places = [], 0, []
    for ref, pieces in zip(chunks, PIECES):
        rows = n * len(pieces)
        copy = pltpu.make_async_copy(ref, g.at[pl.ds(at, rows)], g_sem.at[len(copies)])
        copy.start()
        copies.append((copy, at + rows))
        places += [(at + n * i, p) for i, p in enumerate(pieces)]
        at += rows
    w_copy.wait()
    waited = 0
    group = 4
    for first in range(0, len(places), group):
        inside = places[first:first + group]
        low, high = inside[0][0], inside[-1][0] + n
        while waited < len(copies) and (waited == 0 or copies[waited - 1][1] < high):
            copies[waited][0].wait()
            waited += 1
        product = jnp.dot(g[low:high, :], w[...], preferred_element_type=jnp.float32).astype(jnp.bfloat16)
        for start, (shift, flip, q) in inside:
            x, z = source_of(shift, flip)
            apart = lax.rem(x + row, 2)
            far = lax.rem(x // 2 + row // 2, 2)
            ahead = lax.rem(2 * z + q + 4 - y, 4)
            value = product[start - low:start - low + n]

            @pl.when(apart == 0)
            def _():
                keep[ahead, far] = value

            @pl.when(apart == 1)
            def _():
                send[ahead, far] = value


def grad_input_part(n, chunks, weight):
    ff, d = weight.shape
    rows = 16 * n
    out = jax.ShapeDtypeStruct((4, 2, n, d), jnp.bfloat16)
    return pl.pallas_call(
        functools.partial(grad_input_kernel, n),
        out_shape=(out, out),
        in_specs=[pl.BlockSpec(memory_space=pl.ANY)] * (len(PIECES) + 1),
        out_specs=(pl.BlockSpec(memory_space=pltpu.VMEM),) * 2,
        scratch_shapes=[
            pltpu.VMEM((ff, d), jnp.bfloat16),
            pltpu.VMEM((rows, ff), jnp.bfloat16),
            pltpu.SemaphoreType.DMA,
            pltpu.SemaphoreType.DMA((len(PIECES),)),
        ],
        compiler_params=pltpu.CompilerParams(vmem_limit_bytes=VMEM_LIMIT),
        cost_estimate=pl.CostEstimate(
            flops=2 * rows * ff * d, bytes_accessed=2 * (rows * ff + ff * d + rows * d), transcendentals=0
        ),
    )(*[c.reshape(-1, ff) for c in chunks], weight)


TILE = 256


def grad_weight_kernel(first, last, *refs):
    count = len(PIECES) * len(PARTS)
    chunks, acts_hbm, out = refs[:count], refs[count], refs[-6]
    acts, g, o, in_sem, out_sem = refs[-5:]
    acts_copy = pltpu.make_async_copy(acts_hbm, acts, in_sem.at[0])
    acts_copy.start()
    copies = []
    for tile in range(first, last):
        of_tile, index = [], 0
        for part, (low, n) in enumerate(PARTS):
            for ref, pieces in zip(chunks[part * len(PIECES):], PIECES):
                for i, (shift, flip, q) in enumerate(pieces):
                    x, z = source_of(shift, flip)
                    token = pl.multiple_of((4 * x + 2 * z + q) * BLOCK + low, 32)
                    of_tile.append(
                        pltpu.make_async_copy(
                            ref.at[pl.ds(n * i, n), pl.ds(TILE * tile, TILE)],
                            g.at[tile - first, pl.ds(token, n), :],
                            in_sem.at[1 + index + (tile - first) * 16 * len(PARTS)],
                        )
                    )
                    of_tile[-1].start()
                    index += 1
        copies.append(of_tile)
    acts_copy.wait()
    outs = []
    for tile in range(first, last):
        at = tile - first
        for copy in copies[at]:
            copy.wait()
        o[at] = lax.dot_general(
            g[at], acts[...], (((0,), (0,)), ((), ())), preferred_element_type=jnp.float32
        ).astype(jnp.bfloat16)
        outs.append(pltpu.make_async_copy(o.at[at], out.at[pl.ds(TILE * tile, TILE), :], out_sem.at[at]))
        outs[-1].start()
    for copy in outs:
        copy.wait()


def grad_weight_tiles(first, last, chunks, acts, into):
    ff, d, tokens = chunks[0].shape[-1], acts.shape[1], acts.shape[0]
    tiles = last - first
    args = [c.reshape(-1, ff) for c in chunks] + [acts] + ([] if into is None else [into])
    return pl.pallas_call(
        functools.partial(grad_weight_kernel, first, last),
        out_shape=jax.ShapeDtypeStruct((ff, d), jnp.bfloat16),
        in_specs=[pl.BlockSpec(memory_space=pl.ANY)] * len(args),
        out_specs=pl.BlockSpec(memory_space=pl.ANY),
        scratch_shapes=[
            pltpu.VMEM((tokens, d), jnp.bfloat16),
            pltpu.VMEM((tiles, tokens, TILE), jnp.bfloat16),
            pltpu.VMEM((tiles, TILE, d), jnp.bfloat16),
            pltpu.SemaphoreType.DMA((1 + tiles * 16 * len(PARTS),)),
            pltpu.SemaphoreType.DMA((tiles,)),
        ],
        input_output_aliases={} if into is None else {len(args) - 1: 0},
        compiler_params=pltpu.CompilerParams(vmem_limit_bytes=VMEM_LIMIT),
        cost_estimate=pl.CostEstimate(
            flops=2 * tokens * TILE * tiles * d,
            bytes_accessed=2 * (tokens * TILE * tiles + tokens * d + TILE * tiles * d),
            transcendentals=0,
        ),
    )(*args)


def along_x(value, shift):
    return lax.ppermute(value, "col", [(i, (i + 2 * shift) % 8) for i in range(8)])


def along_z(value):
    return lax.ppermute(value, "col", [(i, i ^ 1) for i in range(8)])


def along_y(value, shift):
    return lax.ppermute(value, "depth", [(i, (i + shift) % 4) for i in range(4)])


def other_core(value):
    return lax.ppermute(value, "row", [(i, i ^ 1) for i in range(4)])


def other_z_hi(value):
    return lax.ppermute(value, "row", [(i, i ^ 2) for i in range(4)])


def gather_part(own):
    left, right, z = along_x(own, 1), along_x(own, -1), along_z(own)
    left2 = along_x(jnp.stack([left[0], z[0]]), 1)
    right2 = along_x(jnp.stack([right[1], z[0]]), -1)
    z2 = along_z(jnp.stack([right[1], left[1]]))
    left3 = along_x(left2[1], 1)
    right3 = along_x(z2[0], -1)
    return [own, left, right, z, left2, right2, z2, left3, right3]


def add(*terms):
    return sum(t.astype(jnp.float32) for t in terms).astype(jnp.bfloat16)


def reduce_part(keep, send):
    got = other_core(send)
    q = [add(keep[i], got[i]) for i in range(4)]
    near = add(q[0], along_y(q[1], 1), along_y(q[2], 2), along_y(q[3], 3))
    return add(near[0], other_z_hi(near[1]))


def shards(activations, grad_output, weight):
    ff = grad_output.shape[1]
    blocks = grad_output.reshape(2, BLOCK, ff)
    acts = lax.all_gather(activations, ("row", "depth"), axis=0, tiled=True)
    gathered, results = [], []
    for low, n in PARTS:
        gathered.append(gather_part(blocks[:, low:low + n]))
    for (low, n), chunks in zip(PARTS, gathered):
        results.append(reduce_part(*grad_input_part(n, chunks, weight)))
    every = gathered[0] + gathered[1]
    tiles = ff // TILE
    weight_grad = grad_weight_tiles(0, 2, every, acts, None)
    weight_grad = grad_weight_tiles(2, tiles, every, acts, weight_grad)
    return jnp.concatenate(results, axis=0), weight_grad


def solution(mesh):
    in_specs = (P(("row", "depth"), "col"), P("col", ("row", "depth")), P(("row", "depth"), "col"))
    out_specs = (P(("row", "depth"), "col"), P(("row", "depth"), "col"))
    return jax.shard_map(shards, mesh=mesh, in_specs=in_specs, out_specs=out_specs, check_vma=False)
```

```python
import functools

import jax
import jax.numpy as jnp
from jax import lax
from jax.experimental import pallas as pl
from jax.experimental.pallas import tpu as pltpu
from jax.sharding import PartitionSpec as P

BLOCK = 192
HINT = 16
PARTS = ((0, 128), (128, 64))
VMEM_LIMIT = 48 * 1024 * 1024
ANY = pl.BlockSpec(memory_space=pl.ANY)

PIECES = (
    ((0, 0, 0), (0, 0, 1)),
    ((3, 0, 0), (3, 0, 1)),
    ((1, 0, 0), (1, 0, 1)),
    ((0, 1, 0), (0, 1, 1)),
    ((2, 0, 0), (3, 1, 0)),
    ((2, 0, 1), (1, 1, 0)),
    ((1, 1, 1), (3, 1, 1)),
    ((2, 1, 0),),
    ((2, 1, 1),),
)


def source_of(shift, flip):
    col = lax.axis_index("col")
    x = lax.rem(col // 2 + shift, 4)
    z = lax.rem(col + flip, 2)
    return x, z


def grad_input_kernel(n, wanted, *refs):
    count = len(wanted)
    chunks, w_hbm = refs[:count], refs[count]
    keep, send = refs[-8:-6]
    w, g, o, w_sem, g_sem, o_sem = refs[-6:]
    row, y = lax.axis_index("row"), lax.axis_index("depth")
    w_copy = pltpu.make_async_copy(w_hbm, w, w_sem)
    w_copy.start()
    copies, at, places = [], 0, []
    for ref, index in zip(chunks, wanted):
        rows = n * len(PIECES[index])
        copy = pltpu.make_async_copy(ref, g.at[pl.ds(at, rows)], g_sem.at[len(copies)])
        copy.start()
        copies.append((copy, at + rows))
        places += [(at + n * i, p) for i, p in enumerate(PIECES[index])]
        at += rows
    w_copy.wait()
    waited, outs = 0, []
    group = 4
    for first in range(0, len(places), group):
        inside = places[first:first + group]
        low, high = inside[0][0], inside[-1][0] + n
        while waited < len(copies) and (waited == 0 or copies[waited - 1][1] < high):
            copies[waited][0].wait()
            waited += 1
        o[low:high, :] = jnp.dot(g[low:high, :], w[...], preferred_element_type=jnp.float32).astype(jnp.bfloat16)
        for start, (shift, flip, q) in inside:
            x, z = source_of(shift, flip)
            apart = lax.rem(x + row, 2)
            far = lax.rem(x // 2 + row // 2, 2)
            ahead = lax.rem(2 * z + q + 4 - y, 4)
            for which, ref in enumerate((keep, send)):
                copy = pltpu.make_async_copy(o.at[pl.ds(start, n)], ref.at[ahead, far], o_sem.at[len(outs) // 2])
                outs.append((apart == which, copy))
                pl.when(apart == which)(copy.start)
    for here, copy in outs:
        pl.when(here)(copy.wait)


def grad_input_part(n, wanted, chunks, weight, into=(), after=()):
    ff, d = weight.shape
    rows = n * sum(len(PIECES[index]) for index in wanted)
    out = jax.ShapeDtypeStruct((4, 2, n, d), jnp.bfloat16)
    args = [chunks[index] for index in wanted] + [weight, *after, *into]
    return pl.pallas_call(
        functools.partial(grad_input_kernel, n, wanted),
        out_shape=(out, out),
        in_specs=[ANY] * len(args),
        out_specs=(ANY,) * 2,
        scratch_shapes=[
            pltpu.VMEM((ff, d), jnp.bfloat16),
            pltpu.VMEM((rows, ff), jnp.bfloat16),
            pltpu.VMEM((rows, d), jnp.bfloat16),
            pltpu.SemaphoreType.DMA,
            pltpu.SemaphoreType.DMA((len(wanted),)),
            pltpu.SemaphoreType.DMA((rows // n,)),
        ],
        input_output_aliases={len(args) - 2 + i: i for i in range(len(into))},
        compiler_params=pltpu.CompilerParams(vmem_limit_bytes=VMEM_LIMIT),
        cost_estimate=pl.CostEstimate(
            flops=2 * rows * ff * d // HINT, bytes_accessed=rows * ff // HINT, transcendentals=0
        ),
    )(*args)


TILE = 256


def grad_weight_kernel(n, first, last, has_sum, final, *refs):
    count = len(PIECES)
    chunks, mine_hbm, other_hbm = refs[:count], refs[count], refs[count + 1]
    sum_hbm = refs[count + 2] if has_sum else None
    out = refs[-9]
    acts, g, total, o, g_sem, a_sem, t_sem, o_sem = refs[-8:]
    row, y = lax.axis_index("row"), lax.axis_index("depth")
    low = sum(m for _, m in PARTS[: [m for _, m in PARTS].index(n)])
    a_copies = []
    for core, ref in enumerate((mine_hbm, other_hbm)):
        for block in range(8):
            copy = pltpu.make_async_copy(
                ref.at[block // 2, block % 2, pl.ds(low, n), :],
                acts.at[pl.ds((core * 8 + block) * n, n), :],
                a_sem.at[core * 8 + block],
            )
            copy.start()
            a_copies.append(copy)
    copies = []
    for tile in range(first, last):
        at = tile - first
        of_tile = []
        for ref, pieces in zip(chunks, PIECES):
            for i, (shift, flip, q) in enumerate(pieces):
                x, z = source_of(shift, flip)
                block = lax.rem(x + row, 2) * 8 + (2 * z + q) * 2 + lax.rem(x // 2 + row // 2, 2)
                of_tile.append(
                    pltpu.make_async_copy(
                        ref.at[pl.ds(n * i, n), pl.ds(TILE * tile, TILE)],
                        g.at[at, pl.ds(pl.multiple_of(block * n, n), n), :],
                        g_sem.at[at * 16 + len(of_tile)],
                    )
                )
                of_tile[-1].start()
        if has_sum:
            of_tile.append(
                pltpu.make_async_copy(sum_hbm.at[pl.ds(TILE * tile, TILE), :], total.at[at], t_sem.at[at])
            )
            of_tile[-1].start()
        copies.append(of_tile)
    for copy in a_copies:
        copy.wait()
    outs = []
    for tile in range(first, last):
        at = tile - first
        for copy in copies[at]:
            copy.wait()
        value = lax.dot_general(g[at], acts[...], (((0,), (0,)), ((), ())), preferred_element_type=jnp.float32)
        if has_sum:
            value = value + total[at]
        if final:
            o[at] = value.astype(jnp.bfloat16)
        else:
            total[at] = value
        outs.append(
            pltpu.make_async_copy(
                (o if final else total).at[at], out.at[pl.ds(TILE * tile, TILE), :], o_sem.at[at]
            )
        )
        outs[-1].start()
    for copy in outs:
        copy.wait()


def grad_weight_tiles(n, first, last, chunks, mine, other, into=None, so_far=None, final=False, after=()):
    ff, d = chunks[0].shape[-1], mine.shape[-1]
    tiles, tokens = last - first, 16 * n
    args = [c.reshape(-1, ff) for c in chunks] + [mine, other] + ([] if so_far is None else [so_far])
    args += list(after) + ([] if into is None else [into])
    return pl.pallas_call(
        functools.partial(grad_weight_kernel, n, first, last, so_far is not None, final),
        out_shape=jax.ShapeDtypeStruct((ff, d), jnp.bfloat16 if final else jnp.float32),
        in_specs=[ANY] * len(args),
        out_specs=ANY,
        scratch_shapes=[
            pltpu.VMEM((tokens, d), jnp.bfloat16),
            pltpu.VMEM((tiles, tokens, TILE), jnp.bfloat16),
            pltpu.VMEM((tiles, TILE, d), jnp.float32),
            pltpu.VMEM((tiles, TILE, d), jnp.bfloat16),
            pltpu.SemaphoreType.DMA((tiles * 16,)),
            pltpu.SemaphoreType.DMA((16,)),
            pltpu.SemaphoreType.DMA((tiles,)),
            pltpu.SemaphoreType.DMA((tiles,)),
        ],
        input_output_aliases={} if into is None else {len(args) - 1: 0},
        compiler_params=pltpu.CompilerParams(vmem_limit_bytes=VMEM_LIMIT),
        cost_estimate=pl.CostEstimate(
            flops=2 * tokens * TILE * tiles * d // HINT,
            bytes_accessed=tokens * TILE * tiles // HINT,
            transcendentals=0,
        ),
    )(*args)


def pack_kernel(places, count, *refs):
    out, sems = refs[-2:]
    copies = []
    for k, (index, start, rows, to) in enumerate(places):
        copies.append(pltpu.make_async_copy(refs[index].at[pl.ds(start, rows)], out.at[pl.ds(to, rows)], sems.at[k]))
        copies[-1].start()
    for copy in copies:
        copy.wait()


def pack(sources, after=()):
    args, places, to = [], [], 0
    for array, start, rows in sources:
        places.append((len(args), start, rows, to))
        args.append(array)
        to += rows
    shape = jax.ShapeDtypeStruct((to, args[0].shape[1]), args[0].dtype)
    return pl.pallas_call(
        functools.partial(pack_kernel, tuple(places), len(args)),
        out_shape=shape,
        in_specs=[ANY] * (len(args) + len(after)),
        out_specs=ANY,
        scratch_shapes=[pltpu.SemaphoreType.DMA((len(places),))],
        cost_estimate=pl.CostEstimate(flops=0, bytes_accessed=4 * shape.size, transcendentals=0),
    )(*args, *after)


def along_x(value, shift):
    return lax.ppermute(value, "col", [(i, (i + 2 * shift) % 8) for i in range(8)])


def along_z(value):
    return lax.ppermute(value, "col", [(i, i ^ 1) for i in range(8)])


def along_y(value, shift):
    return lax.ppermute(value, "depth", [(i, (i + shift) % 4) for i in range(4)])


def other_core(value):
    return lax.ppermute(value, "row", [(i, i ^ 1) for i in range(4)])


def other_z_hi(value):
    return lax.ppermute(value, "row", [(i, i ^ 2) for i in range(4)])


def tie_kernel(*refs):
    pass


def tie(value, after):
    return pl.pallas_call(
        tie_kernel,
        out_shape=jax.ShapeDtypeStruct(value.shape, value.dtype),
        in_specs=[ANY] * (1 + len(after)),
        out_specs=ANY,
        input_output_aliases={0: 0},
        compiler_params=pltpu.CompilerParams(has_side_effects=True),
    )(value, *after)


def first_step(own):
    return along_x(own, 1), along_x(own, -1), along_z(own)


def second_sends(left, right, z):
    n = left.shape[0] // 2
    return (
        jnp.concatenate([left[:n], z[:n]]),
        jnp.concatenate([right[n:], z[:n]]),
        jnp.concatenate([right[n:], left[n:]]),
    )


def second_step(left, right, z):
    return along_x(left, 1), along_x(right, -1), along_z(z)


def third_sends(second, after=()):
    left2, right2, z2 = second
    n = left2.shape[0] // 2
    return pack([(left2, n, n)], after=(right2, *after)), pack([(z2, 0, n)], after=(right2, *after))


def third_step(left, right):
    return along_x(left, 1), along_x(right, -1)


def sum_kernel(groups, *refs):
    outs = refs[len(refs) - len(groups):]
    for out, terms in zip(outs, groups):
        total = None
        for index, at in terms:
            value = (refs[index][...] if at is None else refs[index][at]).astype(jnp.float32)
            total = value if total is None else total + value
        out[...] = total.astype(out.dtype)


def sums(inputs, groups, after=()):
    def shape_of(term):
        return inputs[term[0]].shape if term[1] is None else inputs[term[0]].shape[1:]

    shapes = [jax.ShapeDtypeStruct(shape_of(g[0]), jnp.bfloat16) for g in groups]
    vmem = pl.BlockSpec(memory_space=pltpu.VMEM)
    return pl.pallas_call(
        functools.partial(sum_kernel, groups),
        out_shape=shapes,
        in_specs=[vmem] * len(inputs) + [ANY] * len(after),
        out_specs=[vmem] * len(groups),
        compiler_params=pltpu.CompilerParams(vmem_limit_bytes=VMEM_LIMIT // 2),
    )(*inputs, *after)


def add_cores(keep, got, after=()):
    return sums((keep, got), [((0, i), (1, i)) for i in range(4)], after)


def send_y(q):
    return [along_y(q[i], i) for i in (1, 2, 3)]


def add_y(q, got, after=()):
    return sums((q[0], *got), [tuple((i, k) for i in range(4)) for k in range(2)], after)


def final_kernel(low, n, has_into, near, got, *refs):
    out, value, sem = refs[-3:]
    value[...] = (near[...].astype(jnp.float32) + got[...].astype(jnp.float32)).astype(value.dtype)
    copy = pltpu.make_async_copy(value, out.at[pl.ds(low, n), :], sem)
    copy.start()
    copy.wait()


def final(low, near, got, into=None, after=()):
    n, d = near.shape
    vmem = pl.BlockSpec(memory_space=pltpu.VMEM)
    args = [near, got, *after] + ([] if into is None else [into])
    return pl.pallas_call(
        functools.partial(final_kernel, low, n, into is not None),
        out_shape=jax.ShapeDtypeStruct((BLOCK, d), jnp.bfloat16),
        in_specs=[vmem] * 2 + [ANY] * (len(args) - 2),
        out_specs=ANY,
        scratch_shapes=[pltpu.VMEM((n, d), jnp.bfloat16), pltpu.SemaphoreType.DMA],
        input_output_aliases={} if into is None else {len(args) - 1: 0},
    )(*args)


ALL = tuple(range(len(PIECES)))
EARLY, LATE = ALL[:4], ALL[4:]


def shards(activations, grad_output, weight):
    ff = grad_output.shape[1]
    tiles = ff // TILE
    (low0, n0), (low1, n1) = PARTS

    own0 = pack([(grad_output, low0, n0), (grad_output, BLOCK + low0, n0)])
    first0 = first_step(own0)
    far = other_z_hi(pack([(activations, 0, BLOCK)], after=(own0,)))
    pair = pack([(activations, 0, BLOCK), (far, 0, BLOCK)], after=(own0,))
    mine = lax.all_gather(pair.reshape(2, BLOCK, -1), "depth", axis=0)
    sends = second_sends(*first0)
    second0 = second_step(*sends)
    own1 = pack([(grad_output, low1, n1), (grad_output, BLOCK + low1, n1)], after=sends)
    first1 = first_step(own1)
    third0 = third_step(*third_sends(second0))
    chunks0 = [own0, *first0, *second0, *third0]
    sends = second_sends(*first1)
    second1 = second_step(*sends)
    mine = tie(mine, (*sends, *third0))
    other = other_core(mine)

    keep0, send0 = grad_input_part(n0, ALL, chunks0, weight, after=sends)
    cores0 = other_core(send0)
    so_far = grad_weight_tiles(n0, 0, 4, chunks0, mine, other, after=(keep0,))
    q0 = add_cores(keep0, cores0, after=(so_far,))
    y0 = send_y(q0)
    sends = third_sends(second1, after=(so_far,))
    third1 = third_step(*sends)
    chunks1 = [own1, *first1, *second1, *third1]
    so_far = grad_weight_tiles(n0, 4, tiles, chunks0, mine, other, into=so_far, after=(q0[0], *sends))
    part1 = grad_input_part(n1, EARLY, chunks1, weight, after=(so_far,))
    keep1, send1 = grad_input_part(n1, LATE, chunks1, weight, into=part1)
    cores1 = other_core(send1)
    near0 = add_y(q0, y0, after=(keep1,))
    far0 = other_z_hi(near0[1])
    q1 = add_cores(keep1, cores1, after=(near0[0],))
    y1 = send_y(q1)
    weight_grad = grad_weight_tiles(
        n1, 0, tiles, chunks1, mine, other, so_far=so_far, final=True, after=(q1[0],)
    )
    result = final(low0, near0[0], far0, after=(weight_grad,))
    near1 = add_y(q1, y1, after=(result,))
    far1 = other_z_hi(near1[1])
    result = final(low1, near1[0], far1, into=result)
    return result, weight_grad


def solution(mesh):
    in_specs = (P(("row", "depth"), "col"), P("col", ("row", "depth")), P(("row", "depth"), "col"))
    out_specs = (P(("row", "depth"), "col"), P(("row", "depth"), "col"))
    return jax.shard_map(shards, mesh=mesh, in_specs=in_specs, out_specs=out_specs, check_vma=False)
```

```python
import functools

import jax
import jax.numpy as jnp
from jax import lax
from jax.experimental import pallas as pl
from jax.experimental.pallas import tpu as pltpu
from jax.sharding import PartitionSpec as P

BLOCK = 192
PARTS = ((0,96),(96,96))
MIB = 1024 * 1024
ANY = pl.BlockSpec(memory_space=pl.ANY)

PIECES = (
    ((0, 0, 0), (0, 0, 1)),
    ((3, 0, 0), (3, 0, 1)),
    ((1, 0, 0), (1, 0, 1)),
    ((0, 1, 0), (0, 1, 1)),
    ((2, 0, 0), (3, 1, 0)),
    ((2, 0, 1), (1, 1, 0)),
    ((1, 1, 1), (3, 1, 1)),
    ((2, 1, 0),),
    ((2, 1, 1),),
)


def source_of(shift, flip):
    col = lax.axis_index("col")
    x = lax.rem(col // 2 + shift, 4)
    z = lax.rem(col + flip, 2)
    return x, z


def grad_input_kernel(n, wanted, split, *refs):
    count = len(wanted)
    chunks, w_hbm = refs[:count], refs[count]
    keep, sends = refs[-7 - split], refs[-6 - split:-6]
    w, g, o, w_sem, g_sem, o_sem = refs[-6:]
    row, y = lax.axis_index("row"), lax.axis_index("depth")
    w_copy = pltpu.make_async_copy(w_hbm, w, w_sem)
    w_copy.start()
    copies, at, places = [], 0, []
    for ref, index in zip(chunks, wanted):
        rows = n * len(PIECES[index])
        copy = pltpu.make_async_copy(ref, g.at[pl.ds(at, rows)], g_sem.at[len(copies)])
        copy.start()
        copies.append((copy, at + rows))
        places += [(at + n * i, p) for i, p in enumerate(PIECES[index])]
        at += rows
    w_copy.wait()
    waited, done, outs = 0, 0, []
    group = 4
    for first in range(0, len(places), group):
        inside = places[first:first + group]
        low, high = inside[0][0], inside[-1][0] + n
        while waited < len(copies) and (waited == 0 or copies[waited - 1][1] < high):
            copies[waited][0].wait()
            waited += 1
        o[low:high, :] = jnp.dot(g[low:high, :], w[...], preferred_element_type=jnp.float32).astype(jnp.bfloat16)
        for start, (shift, flip, q) in inside:
            x, z = source_of(shift, flip)
            apart = lax.rem(x + row, 2)
            far = lax.rem(x // 2 + row // 2, 2)
            ahead = lax.rem(2 * z + q + 4 - y, 4)
            each = 4 // split
            targets = [(apart == 0, keep.at[ahead, far])]
            for k, ref in enumerate(sends):
                targets.append(((apart == 1) & (ahead // each == k), ref.at[lax.rem(ahead, each), far]))
            for here, ref in targets:
                copy = pltpu.make_async_copy(o.at[pl.ds(start, n)], ref, o_sem.at[done])
                outs.append((here, copy))
                pl.when(here)(copy.start)
            done += 1
    for here, copy in outs:
        pl.when(here)(copy.wait)


def grad_input_part(n, wanted, split, chunks, weight, into=(), after=()):
    ff, d = weight.shape
    rows = n * sum(len(PIECES[index]) for index in wanted)
    shapes = [jax.ShapeDtypeStruct((count, 2, n, d), jnp.bfloat16) for count in [4] + [4 // split] * split]
    args = [chunks[index] for index in wanted] + [weight, *after, *into]
    return pl.pallas_call(
        functools.partial(grad_input_kernel, n, wanted, split),
        out_shape=shapes,
        in_specs=[ANY] * len(args),
        out_specs=[ANY] * len(shapes),
        scratch_shapes=[
            pltpu.VMEM((ff, d), jnp.bfloat16),
            pltpu.VMEM((rows, ff), jnp.bfloat16),
            pltpu.VMEM((rows, d), jnp.bfloat16),
            pltpu.SemaphoreType.DMA,
            pltpu.SemaphoreType.DMA((len(wanted),)),
            pltpu.SemaphoreType.DMA((rows // n,)),
        ],
        input_output_aliases={len(args) - len(into) + i: i for i in range(len(into))},
        compiler_params=pltpu.CompilerParams(vmem_limit_bytes=20 * MIB),
        cost_estimate=pl.CostEstimate(
            flops=2 * rows * ff * d , bytes_accessed=rows * ff , transcendentals=0
        ),
    )(*args)


TILE = 256


def grad_weight_kernel(first, last, *refs):
    count = len(PIECES) * len(PARTS)
    chunks, acts_hbm, out = refs[:count], refs[count], refs[-7]
    acts, g, o, a_sem, g_sem, o_sem = refs[-6:]
    row = lax.axis_index("row")
    acts_copy = pltpu.make_async_copy(acts_hbm, acts, a_sem)
    acts_copy.start()
    copies = []
    for tile in range(first, last):
        at, of_tile = tile - first, []
        for part, (low, n) in enumerate(PARTS):
            for ref, pieces in zip(chunks[part * len(PIECES):], PIECES):
                for i, (shift, flip, q) in enumerate(pieces):
                    x, z = source_of(shift, flip)
                    block = lax.rem(x, 2) * 8 + (2 * z + q) * 2 + lax.rem(x // 2 + row // 2, 2)
                    of_tile.append(
                        pltpu.make_async_copy(
                            ref.at[pl.ds(n * i, n), pl.ds(TILE * tile, TILE)],
                            g.at[at, pl.ds(pl.multiple_of(block * BLOCK + low, 16), n), :],
                            g_sem.at[at * 16 * len(PARTS) + len(of_tile)],
                        )
                    )
                    of_tile[-1].start()
        copies.append(of_tile)
    acts_copy.wait()
    outs = []
    for tile in range(first, last):
        at = tile - first
        for copy in copies[at]:
            copy.wait()
        o[at] = lax.dot_general(
            g[at], acts[...], (((0,), (0,)), ((), ())), preferred_element_type=jnp.float32
        ).astype(jnp.bfloat16)
        outs.append(pltpu.make_async_copy(o.at[at], out.at[pl.ds(TILE * tile, TILE), :], o_sem.at[at]))
        outs[-1].start()
    for copy in outs:
        copy.wait()


def grad_weight_tiles(first, last, chunks, acts, into=None, after=()):
    ff, (tokens, d) = chunks[0].shape[-1], acts.shape
    tiles = last - first
    args = [*chunks, acts, *after] + ([] if into is None else [into])
    return pl.pallas_call(
        functools.partial(grad_weight_kernel, first, last),
        out_shape=jax.ShapeDtypeStruct((ff, d), jnp.bfloat16),
        in_specs=[ANY] * len(args),
        out_specs=ANY,
        scratch_shapes=[
            pltpu.VMEM((tokens, d), jnp.bfloat16),
            pltpu.VMEM((tiles, tokens, TILE), jnp.bfloat16),
            pltpu.VMEM((tiles, TILE, d), jnp.bfloat16),
            pltpu.SemaphoreType.DMA,
            pltpu.SemaphoreType.DMA((tiles * 16 * len(PARTS),)),
            pltpu.SemaphoreType.DMA((tiles,)),
        ],
        input_output_aliases={} if into is None else {len(args) - 1: 0},
        compiler_params=pltpu.CompilerParams(vmem_limit_bytes=24 * MIB),
        cost_estimate=pl.CostEstimate(
            flops=2 * tokens * TILE * tiles * d,
            bytes_accessed=2 * (tokens * TILE * tiles + tokens * d + TILE * tiles * d),
            transcendentals=0,
        ),
    )(*args)


def pack_kernel(places, count, *refs):
    out, sems = refs[-2:]
    copies = []
    for k, (index, start, rows, to) in enumerate(places):
        copies.append(pltpu.make_async_copy(refs[index].at[pl.ds(start, rows)], out.at[pl.ds(to, rows)], sems.at[k]))
        copies[-1].start()
    for copy in copies:
        copy.wait()


def pack(sources, after=()):
    args, places, to = [], [], 0
    for array, start, rows in sources:
        places.append((len(args), start, rows, to))
        args.append(array)
        to += rows
    shape = jax.ShapeDtypeStruct((to, args[0].shape[1]), args[0].dtype)
    return pl.pallas_call(
        functools.partial(pack_kernel, tuple(places), len(args)),
        out_shape=shape,
        in_specs=[ANY] * (len(args) + len(after)),
        out_specs=pl.BlockSpec(memory_space=pltpu.VMEM),
        scratch_shapes=[pltpu.SemaphoreType.DMA((len(places),))],
        cost_estimate=pl.CostEstimate(flops=0, bytes_accessed=4 * shape.size, transcendentals=0),
    )(*args, *after)


def along_x(value, shift):
    return lax.ppermute(value, "col", [(i, (i + 2 * shift) % 8) for i in range(8)])


def along_z(value):
    return lax.ppermute(value, "col", [(i, i ^ 1) for i in range(8)])


def along_y(value, shift):
    return lax.ppermute(value, "depth", [(i, (i + shift) % 4) for i in range(4)])


def other_core(value):
    return lax.ppermute(value, "row", [(i, i ^ 1) for i in range(4)])


def other_z_hi(value):
    return lax.ppermute(value, "row", [(i, i ^ 2) for i in range(4)])


def tie_kernel(*refs):
    pass


def tie(value, after):
    return pl.pallas_call(
        tie_kernel,
        out_shape=jax.ShapeDtypeStruct(value.shape, value.dtype),
        in_specs=[ANY] * (1 + len(after)),
        out_specs=ANY,
        input_output_aliases={0: 0},
        compiler_params=pltpu.CompilerParams(has_side_effects=True),
    )(value, *after)


def first_step(own):
    return along_x(own, 1), along_x(own, -1), along_z(own)


def second_sends(left, right, z, after=()):
    n = left.shape[0] // 2
    return (
        pack([(left, 0, n), (z, 0, n)], after),
        pack([(right, n, n), (z, 0, n)], after),
        pack([(right, n, n), (left, n, n)], after),
    )


def second_step(left, right, z):
    return along_x(left, 1), along_x(right, -1), along_z(z)


def third_sends(second, after=()):
    left2, right2, z2 = second
    n = left2.shape[0] // 2
    return pack([(left2, n, n)], after=(right2, *after)), pack([(z2, 0, n)], after=(right2, *after))


def third_step(left, right):
    return along_x(left, 1), along_x(right, -1)


def sum_kernel(groups, *refs):
    outs = refs[len(refs) - len(groups):]
    for out, terms in zip(outs, groups):
        total = None
        for index, at in terms:
            value = (refs[index][...] if at is None else refs[index][at]).astype(jnp.float32)
            total = value if total is None else total + value
        out[...] = total.astype(out.dtype)


def sums(inputs, groups, after=()):
    def shape_of(term):
        return inputs[term[0]].shape if term[1] is None else inputs[term[0]].shape[1:]

    shapes = [jax.ShapeDtypeStruct(shape_of(g[0]), jnp.bfloat16) for g in groups]
    vmem = pl.BlockSpec(memory_space=pltpu.VMEM)
    return pl.pallas_call(
        functools.partial(sum_kernel, groups),
        out_shape=shapes,
        in_specs=[vmem] * len(inputs) + [ANY] * len(after),
        out_specs=[vmem] * len(groups),
        compiler_params=pltpu.CompilerParams(vmem_limit_bytes=16 * MIB),
    )(*inputs, *after)


def add_cores(keep, got, after=()):
    each = 4 // len(got)
    return sums((keep, *got), [((0, i), (1 + i // each, i % each)) for i in range(4)], after)


def send_y(q):
    return [along_y(q[i], i) for i in (1, 2, 3)]


def add_y(q, got, after=()):
    return sums((q[0], *got), [tuple((i, k) for i in range(4)) for k in range(2)], after)


def final_kernel(low, n, has_into, near, got, *refs):
    out, value, sem = refs[-3:]
    value[...] = (near[...].astype(jnp.float32) + got[...].astype(jnp.float32)).astype(value.dtype)
    copy = pltpu.make_async_copy(value, out.at[pl.ds(low, n), :], sem)
    copy.start()
    copy.wait()


def final(low, near, got, into=None, after=()):
    n, d = near.shape
    vmem = pl.BlockSpec(memory_space=pltpu.VMEM)
    args = [near, got, *after] + ([] if into is None else [into])
    return pl.pallas_call(
        functools.partial(final_kernel, low, n, into is not None),
        out_shape=jax.ShapeDtypeStruct((BLOCK, d), jnp.bfloat16),
        in_specs=[vmem] * 2 + [ANY] * (len(args) - 2),
        out_specs=ANY,
        scratch_shapes=[pltpu.VMEM((n, d), jnp.bfloat16), pltpu.SemaphoreType.DMA],
        input_output_aliases={} if into is None else {len(args) - 1: 0},
    )(*args)


ALL = tuple(range(len(PIECES)))
EARLY, LATE = ALL[:7], ALL[7:]
SAME_CHIP = [[0, 1], [2, 3]]


def shards(activations, grad_output, weight):
    ff = grad_output.shape[1]
    tiles, d = ff // TILE, weight.shape[1]
    (low0, n0), (low1, n1) = PARTS

    own0 = pack([(grad_output, low0, n0), (grad_output, BLOCK + low0, n0)])
    first0 = first_step(own0)
    far = other_z_hi(activations)
    pair = pack([(activations, 0, BLOCK), (far, 0, BLOCK)], after=first0)
    acts = lax.all_gather(pair, "depth", axis=0, tiled=True)
    sends = second_sends(*first0)
    second0 = second_step(*sends)
    own1 = pack([(grad_output, low1, n1), (grad_output, BLOCK + low1, n1)], after=sends)
    first1 = first_step(own1)
    sends = third_sends(second0)
    third0 = third_step(*sends)
    chunks0 = [own0, *first0, *second0, *third0]

    part0 = grad_input_part(n0, EARLY, 2, chunks0, weight, after=(own1, *sends))
    keep0, *send0 = grad_input_part(n0, LATE, 2, chunks0, weight, into=part0)
    cores0 = [other_core(v) for v in send0]
    second1 = second_step(*second_sends(*first1, after=(keep0,)))
    q0 = add_cores(keep0, cores0)
    y0 = send_y(q0)
    sends = third_sends(second1, after=(q0[0],))
    third1 = third_step(*sends)
    chunks1 = [own1, *first1, *second1, *third1]
    acts = tie(acts, sends)
    part1 = grad_input_part(n1, EARLY, 2, chunks1, weight, after=(q0[0], acts))
    acts = lax.all_gather(acts, "row", axis=0, tiled=True, axis_index_groups=SAME_CHIP)
    near0 = add_y(q0, y0, after=(part1[0],))
    far0 = other_z_hi(near0[1])
    keep1, *send1 = grad_input_part(n1, LATE, 2, chunks1, weight, into=part1, after=(near0[0],))
    cores1 = [other_core(v) for v in send1]
    chunks = chunks0 + chunks1
    weight_grad = grad_weight_tiles(0, 1, chunks, acts, after=(keep1,))
    q1 = add_cores(keep1, cores1, after=(weight_grad,))
    y1 = send_y(q1)
    weight_grad = grad_weight_tiles(1, 6, chunks, acts, into=weight_grad, after=(q1[0],))
    result = final(low0, near0[0], far0, after=(weight_grad,))
    near1 = add_y(q1, y1, after=(result,))
    far1 = other_z_hi(near1[1])
    weight_grad = grad_weight_tiles(6, tiles, chunks, acts, into=weight_grad, after=(near1[0],))
    result = final(low1, near1[0], far1, into=result, after=(weight_grad,))
    return result, weight_grad


def solution(mesh):
    in_specs = (P(("row", "depth"), "col"), P("col", ("row", "depth")), P(("row", "depth"), "col"))
    out_specs = (P(("row", "depth"), "col"), P(("row", "depth"), "col"))
    return jax.shard_map(shards, mesh=mesh, in_specs=in_specs, out_specs=out_specs, check_vma=False)
```

```python
import functools

import jax
import jax.numpy as jnp
from jax import lax
from jax.experimental import pallas as pl
from jax.experimental.pallas import tpu as pltpu
from jax.sharding import PartitionSpec as P

BLOCK = 192
PARTS = ((0, BLOCK),)
MIB = 1024 * 1024
ANY = pl.BlockSpec(memory_space=pltpu.HBM)

PIECES = (
    ((0, 0, 0), (0, 0, 1)),
    ((3, 0, 0), (3, 0, 1)),
    ((1, 0, 0), (1, 0, 1)),
    ((0, 1, 0), (0, 1, 1)),
    ((2, 0, 0), (3, 1, 0)),
    ((2, 0, 1), (1, 1, 0)),
    ((1, 1, 1), (3, 1, 1)),
    ((2, 1, 0),),
    ((2, 1, 1),),
)


def source_of(shift, flip):
    col = lax.axis_index("col")
    x = lax.rem(col // 2 + shift, 4)
    z = lax.rem(col + flip, 2)
    return x, z


def grad_input_kernel(n, wanted, split, *refs):
    count = len(wanted)
    chunks, w_hbm = refs[:count], refs[count]
    keep, sends = refs[-7 - split], refs[-6 - split:-6]
    w, g, o, w_sem, g_sem, o_sem = refs[-6:]
    row, y = lax.axis_index("row"), lax.axis_index("depth")
    w_copy = pltpu.make_async_copy(w_hbm, w, w_sem)
    w_copy.start()
    copies, at, places = [], 0, []
    for ref, index in zip(chunks, wanted):
        rows = n * len(PIECES[index])
        copy = pltpu.make_async_copy(ref, g.at[pl.ds(at, rows)], g_sem.at[len(copies)])
        copy.start()
        copies.append((copy, at + rows))
        places += [(at + n * i, p) for i, p in enumerate(PIECES[index])]
        at += rows
    w_copy.wait()
    waited, done, outs = 0, 0, []
    group = 4
    for first in range(0, len(places), group):
        inside = places[first:first + group]
        low, high = inside[0][0], inside[-1][0] + n
        while waited < len(copies) and (waited == 0 or copies[waited - 1][1] < high):
            copies[waited][0].wait()
            waited += 1
        o[low:high, :] = jnp.dot(g[low:high, :], w[...], preferred_element_type=jnp.float32).astype(jnp.bfloat16)
        for start, (shift, flip, q) in inside:
            x, z = source_of(shift, flip)
            apart = lax.rem(x + row, 2)
            far = lax.rem(x // 2 + row // 2, 2)
            ahead = lax.rem(2 * z + q + 4 - y, 4)
            each = 4 // split
            targets = [(apart == 0, keep.at[ahead, far])]
            for k, ref in enumerate(sends):
                targets.append(((apart == 1) & (ahead // each == k), ref.at[lax.rem(ahead, each), far]))
            for here, ref in targets:
                copy = pltpu.make_async_copy(o.at[pl.ds(start, n)], ref, o_sem.at[done])
                outs.append((here, copy))
                pl.when(here)(copy.start)
            done += 1
    for here, copy in outs:
        pl.when(here)(copy.wait)


def grad_input_part(n, wanted, split, chunks, weight, into=(), after=()):
    ff, d = weight.shape
    rows = n * sum(len(PIECES[index]) for index in wanted)
    shapes = [jax.ShapeDtypeStruct((count, 2, n, d), jnp.bfloat16) for count in [4] + [4 // split] * split]
    args = [chunks[index] for index in wanted] + [weight, *after, *into]
    return pl.pallas_call(
        functools.partial(grad_input_kernel, n, wanted, split),
        out_shape=shapes,
        in_specs=[ANY] * len(args),
        out_specs=[ANY] * len(shapes),
        scratch_shapes=[
            pltpu.VMEM((ff, d), jnp.bfloat16),
            pltpu.VMEM((rows, ff), jnp.bfloat16),
            pltpu.VMEM((rows, d), jnp.bfloat16),
            pltpu.SemaphoreType.DMA,
            pltpu.SemaphoreType.DMA((len(wanted),)),
            pltpu.SemaphoreType.DMA((rows // n,)),
        ],
        input_output_aliases={len(args) - len(into) + i: i for i in range(len(into))},
        compiler_params=pltpu.CompilerParams(vmem_limit_bytes=60 * MIB),
        cost_estimate=pl.CostEstimate(
            flops=2 * rows * ff * d , bytes_accessed=rows * ff , transcendentals=0
        ),
    )(*args)


TILE = 256


def grad_weight_kernel(first, last, *refs):
    count = len(PIECES) * len(PARTS)
    chunks, acts_hbm, out = refs[:count], refs[count], refs[-7]
    acts, g, o, a_sem, g_sem, o_sem = refs[-6:]
    acts_copy = pltpu.make_async_copy(acts_hbm, acts, a_sem)
    acts_copy.start()
    copies = []
    for tile in range(first, last):
        at, of_tile = tile - first, []
        for part, (low, n) in enumerate(PARTS):
            for ref, pieces in zip(chunks[part * len(PIECES):], PIECES):
                for i, (shift, flip, q) in enumerate(pieces):
                    x, z = source_of(shift, flip)
                    block = 4 * x + 2 * z + q
                    of_tile.append(
                        pltpu.make_async_copy(
                            ref.at[pl.ds(n * i, n), pl.ds(TILE * tile, TILE)],
                            g.at[at, pl.ds(pl.multiple_of(block * BLOCK + low, 16), n), :],
                            g_sem.at[at * 16 * len(PARTS) + len(of_tile)],
                        )
                    )
                    of_tile[-1].start()
        copies.append(of_tile)
    acts_copy.wait()
    outs = []
    for tile in range(first, last):
        at = tile - first
        for copy in copies[at]:
            copy.wait()
        o[at] = lax.dot_general(
            g[at], acts[...], (((0,), (0,)), ((), ())), preferred_element_type=jnp.float32
        ).astype(jnp.bfloat16)
        outs.append(pltpu.make_async_copy(o.at[at], out.at[pl.ds(TILE * tile, TILE), :], o_sem.at[at]))
        outs[-1].start()
    for copy in outs:
        copy.wait()


def grad_weight_tiles(first, last, chunks, acts, into=None, after=()):
    ff, (tokens, d) = chunks[0].shape[-1], acts.shape
    tiles = last - first
    args = [*chunks, acts, *after] + ([] if into is None else [into])
    return pl.pallas_call(
        functools.partial(grad_weight_kernel, first, last),
        out_shape=jax.ShapeDtypeStruct((ff, d), jnp.bfloat16),
        in_specs=[ANY] * len(args),
        out_specs=ANY,
        scratch_shapes=[
            pltpu.VMEM((tokens, d), jnp.bfloat16),
            pltpu.VMEM((tiles, tokens, TILE), jnp.bfloat16),
            pltpu.VMEM((tiles, TILE, d), jnp.bfloat16),
            pltpu.SemaphoreType.DMA,
            pltpu.SemaphoreType.DMA((tiles * 16 * len(PARTS),)),
            pltpu.SemaphoreType.DMA((tiles,)),
        ],
        input_output_aliases={} if into is None else {len(args) - 1: 0},
        compiler_params=pltpu.CompilerParams(vmem_limit_bytes=60 * MIB),
        cost_estimate=pl.CostEstimate(
            flops=2 * tokens * TILE * tiles * d,
            bytes_accessed=2 * (tokens * TILE * tiles + tokens * d + TILE * tiles * d),
            transcendentals=0,
        ),
    )(*args)


def along_x(value, shift):
    return lax.ppermute(value, "col", [(i, (i + 2 * shift) % 8) for i in range(8)])


def along_z(value):
    return lax.ppermute(value, "col", [(i, i ^ 1) for i in range(8)])


def along_y(value, shift):
    return lax.ppermute(value, "depth", [(i, (i + shift) % 4) for i in range(4)])


def other_core(value):
    return lax.ppermute(value, "row", [(i, i ^ 1) for i in range(4)])


def other_z_hi(value):
    return lax.ppermute(value, "row", [(i, i ^ 2) for i in range(4)])


def first_step(own):
    return along_x(own, 1), along_x(own, -1), along_z(own)


def second_sends(left, right, z):
    n = left.shape[0] // 2
    return (
        jnp.concatenate([left[:n], z[:n]]),
        jnp.concatenate([right[n:], z[:n]]),
        jnp.concatenate([right[n:], left[n:]]),
    )


def second_step(left, right, z):
    return along_x(left, 1), along_x(right, -1), along_z(z)


def rows_kernel(start, *refs):
    out, sem = refs[-2:]
    copy = pltpu.make_async_copy(refs[0].at[pl.ds(start, out.shape[0])], out, sem)
    copy.start()
    copy.wait()


def rows_of(value, start, count, after):
    return pl.pallas_call(
        functools.partial(rows_kernel, start),
        out_shape=jax.ShapeDtypeStruct((count, value.shape[1]), value.dtype),
        in_specs=[ANY] * (1 + len(after)),
        out_specs=pl.BlockSpec(memory_space=pltpu.VMEM),
        scratch_shapes=[pltpu.SemaphoreType.DMA],
        compiler_params=pltpu.CompilerParams(vmem_limit_bytes=60 * MIB),
    )(value, *after)


def third_sends(left2, z2, after):
    n = left2.shape[0] // 2
    return rows_of(left2, n, n, after), rows_of(z2, 0, n, after)


def third_step(left, right):
    return along_x(left, 1), along_x(right, -1)


HALF = BLOCK // 2


def wide(value):
    return value.astype(jnp.float32)


def cores_kernel(keep, got, *refs):
    own_y, *to_y, own_z, to_z = refs[-6:]
    for i in range(4):
        for far in range(2):
            total = (wide(keep[i, far]) + wide(got[i, far])).astype(jnp.bfloat16)
            (to_y[i - 1] if i else own_y)[far] = total[:HALF]
            (to_z if far else own_z)[i] = total[HALF:]


def first_sums_kernel(own_y, got1, got2, got3, own_z, got_z, *refs):
    near, to_far, at0, at1, at2, at3 = refs[-6:]
    for far, out in enumerate((near, to_far)):
        out[...] = (
            wide(own_y[far]) + wide(got1[far]) + wide(got2[far]) + wide(got3[far])
        ).astype(jnp.bfloat16)
    for i, out in enumerate((at0, at1, at2, at3)):
        out[...] = (wide(own_z[i]) + wide(got_z[i])).astype(jnp.bfloat16)


def last_sums_kernel(near, got_far, at0, got1, got2, got3, *refs):
    out = refs[-1]
    out[:HALF, :] = (wide(near[...]) + wide(got_far[...])).astype(jnp.bfloat16)
    out[HALF:, :] = (wide(at0[...]) + wide(got1[...]) + wide(got2[...]) + wide(got3[...])).astype(jnp.bfloat16)


def in_vmem(kernel, inputs, shapes, after=()):
    vmem = pl.BlockSpec(memory_space=pltpu.VMEM)
    return pl.pallas_call(
        kernel,
        out_shape=[jax.ShapeDtypeStruct(shape, jnp.bfloat16) for shape in shapes],
        in_specs=[vmem] * len(inputs) + [ANY] * len(after),
        out_specs=[vmem] * len(shapes),
        compiler_params=pltpu.CompilerParams(vmem_limit_bytes=60 * MIB),
    )(*inputs, *after)


def shards(activations, grad_output, weight):
    tiles, d = grad_output.shape[1] // TILE, weight.shape[1]
    acts = lax.all_gather(activations, ("row", "depth"), axis=0, tiled=True)

    first = first_step(grad_output)
    sends = second_sends(*first)
    second = second_step(*sends)
    chunks = [grad_output, *first]
    part = grad_input_part(BLOCK, (0, 1, 2, 3), 1, chunks, weight, after=sends)
    sends = third_sends(second[0], second[2], (part[0],))
    third = third_step(*sends)
    chunks += [*second, *third]
    part = grad_input_part(BLOCK, (4, 5, 6), 1, chunks, weight, into=part, after=sends)
    keep, send = grad_input_part(BLOCK, (7, 8), 1, chunks, weight, into=part)

    got = other_core(send)
    weight_grad = grad_weight_tiles(0, 2, chunks, acts, after=(keep,))
    halves = [(2, HALF, d)] * 4 + [(4, HALF, d)] * 2
    own_y, *to_y, own_z, to_z = in_vmem(cores_kernel, (keep, got), halves, after=(weight_grad,))
    got_y = [along_y(to_y[i - 1], i) for i in (1, 2, 3)]
    got_z = other_z_hi(to_z)
    weight_grad = grad_weight_tiles(2, 5, chunks, acts, into=weight_grad, after=(own_y,))
    near, to_far, *at = in_vmem(
        first_sums_kernel, (own_y, *got_y, own_z, got_z), [(HALF, d)] * 6, after=(weight_grad,)
    )
    got_far = other_z_hi(to_far)
    got_y = [along_y(at[i], i) for i in (1, 2, 3)]
    weight_grad = grad_weight_tiles(5, tiles, chunks, acts, into=weight_grad, after=(near,))
    (result,) = in_vmem(
        last_sums_kernel, (near, got_far, at[0], *got_y), [(BLOCK, d)], after=(weight_grad,)
    )
    return result, weight_grad


def solution(mesh):
    in_specs = (P(("row", "depth"), "col"), P("col", ("row", "depth")), P(("row", "depth"), "col"))
    out_specs = (P(("row", "depth"), "col"), P(("row", "depth"), "col"))
    return jax.shard_map(shards, mesh=mesh, in_specs=in_specs, out_specs=out_specs, check_vma=False)
```
